256 devices in a mesh: section: 2 (over core), kv: 32 (over z, x), head: 4 (over y).
Axes of the slice: x: 4, y: 4, z: 8, core: 2. Of those that a mesh axis runs over, the one named last changes fastest.
Arguments:
- queries: bfloat16 [16, 128, 576], P('section', 'head'), may hold values from -180 to 180
- cache: bfloat16 [4096, 128, 576], P(('section', 'kv')), may hold values from -8 to 8
- slot_request: int32 [4096], P(('section', 'kv')), may hold values from -1 to 15, as said below
- slot_page: int32 [4096], P(('section', 'kv')), may hold values from 0 to 255
- lengths: int32 [16], P('section'), may hold values from 4096 to 32768, as said below
- w_uv: bfloat16 [128, 512, 128], P('head'), may hold values from -3 to 3
- w_out: bfloat16 [16384, 7168], P('head', ('section', 'kv')), may hold values from -0.046875 to 0.046875
- hidden: bfloat16 [16, 7168], P(None, ('section', 'kv')), may hold values from -6 to 6
Outputs:
- mixed: bfloat16 [16, 7168], P(None, ('section', 'kv'))
The draws below stay inside these ranges and needn't reach their ends.
Inputs may be any that keep to these rules, and one draw needn't show every extreme that they name: `slot_request`: requests b with b // 8 = i have their pages only in slots of index i of section; each such request owns exactly one slot for each page number below ceil(lengths[b] / 128) and no other; the remaining slots are -1. `lengths`: in every index of section one request holds exactly 32768 tokens.
All inputs are finite; a program needn't handle non-finite values.
Results may differ from the reference program's by a relative error of at most 0.015.
Values may be sent and summed in bfloat16 or wider, within the bound.
No kernel may reach another device: no remote copies, remote signals or barrier semaphores. Data moves between devices by JAX's collectives and lax.ppermute only.
A program may use at most 128 MiB of HBM per device.

```python
import jax
import jax.numpy as jnp
from jax import lax

D = 7168
HEADS = 128
LAT = 512
ROPE = 64
NOPE = 128
VDIM = 128
PAGE = 128
RQ = 8
BATCH = 16
SLOTS = 4096
MAX_PAGES = 256
MAX_LEN = 32768


def page_layout(key):
    sections = BATCH // RQ
    per_section = SLOTS // sections
    key_len, key_top, key_perm = jax.random.split(jax.random.fold_in(key, 100), 3)
    lowest = max(MAX_LEN // 8, 1)
    request_lengths = jax.random.randint(key_len, (sections, RQ), lowest, MAX_LEN + 1)
    longest = jax.random.randint(key_top, (sections,), 0, RQ)
    request_lengths = jnp.where(jnp.arange(RQ)[None, :] == longest[:, None], MAX_LEN, request_lengths)
    entries = jnp.arange(per_section)
    owner_local = entries // MAX_PAGES
    numbers = entries % MAX_PAGES
    live = numbers[None, :] * PAGE < jnp.take(request_lengths, owner_local, axis=1)
    owner_global = owner_local[None, :] + RQ * jnp.arange(sections)[:, None]
    owners = jnp.where(live, owner_global, -1)
    orders = jax.vmap(lambda part_key: jax.random.permutation(part_key, per_section))(jax.random.split(key_perm, sections))
    slot_owner = jnp.take_along_axis(owners, orders, axis=1).reshape(-1).astype(jnp.int32)
    numbers_all = jnp.broadcast_to(numbers[None, :], (sections, per_section))
    slot_number = jnp.take_along_axis(numbers_all, orders, axis=1).reshape(-1).astype(jnp.int32)
    return (request_lengths.reshape(-1).astype(jnp.int32), slot_owner, slot_number)


def draw_lengths(key, part):
    return page_layout(key)[0]


def draw_slot_request(key, part):
    return page_layout(key)[1]


def draw_slot_page(key, part):
    return page_layout(key)[2]


def draw_cache(key, part):
    key = jax.random.fold_in(key, 1)
    values = jnp.clip(jax.random.normal(key, (SLOTS, PAGE, LAT + ROPE), jnp.float32), -6.0, 6.0)
    return values.astype(jnp.bfloat16)


def draw_queries(key, part):
    key = jax.random.fold_in(key, 2)
    key_main = jax.random.fold_in(key, 0)
    values = jnp.clip(jax.random.normal(key_main, (BATCH, HEADS, LAT + ROPE), jnp.float32), -6.0, 6.0)
    return values.astype(jnp.bfloat16)


def block_levels(own_key, shape, cuts, smallest, top_value):
    gain = 1.0
    for axis_at, blocks in cuts:
        draws = jax.random.uniform(jax.random.fold_in(jax.random.fold_in(own_key, 6), axis_at), (blocks,), jnp.float32, smallest / len(cuts), top_value / len(cuts))
        gain = gain * jnp.repeat(jnp.exp(draws), shape[axis_at] // blocks).reshape((-1,) + (1,) * (len(shape) - 1 - axis_at))
    return gain


def centred(key, shape, scale, most, shards=(), kind=jnp.bfloat16):
    drawn = scale * jax.random.normal(key, shape, jnp.float32)
    if shards:
        drawn = drawn * block_levels(key, shape, shards, -0.22, 0.18)
    return jnp.clip(drawn, -most, most).astype(kind)


def setup_inputs(seed: int = 0) -> dict:
    streams_of = jax.random.split(jax.random.key(seed), 9)
    return {
        "queries": draw_queries(jax.random.fold_in(streams_of[8], 71), 0),
        "cache": draw_cache(jax.random.fold_in(streams_of[8], 71), 0),
        "slot_request": draw_slot_request(jax.random.fold_in(streams_of[8], 71), 0),
        "slot_page": draw_slot_page(jax.random.fold_in(streams_of[8], 71), 0),
        "lengths": draw_lengths(jax.random.fold_in(streams_of[8], 71), 0),
        "w_uv": centred(streams_of[5], (HEADS, LAT, VDIM), 0.5, 3.0, ((0, 4),)),
        "w_out": centred(streams_of[6], (HEADS * VDIM, D), (HEADS * VDIM) ** -0.5, 0.046875, ((0, 4), (1, 64))),
        "hidden": centred(streams_of[7], (BATCH, D), 1.0, 6.0, ((1, 64),)),
    }


def reference(queries, cache, slot_request, slot_page, lengths, w_uv, w_out, hidden):
    scale = (NOPE + ROPE) ** -0.5
    per_section = SLOTS // (BATCH // RQ)
    offsets = jnp.arange(PAGE).astype(jnp.int32)

    def one_request(request):
        start = ((request // RQ) * per_section).astype(jnp.int32)
        owners = lax.dynamic_slice_in_dim(slot_request, start, per_section)
        numbers = lax.dynamic_slice_in_dim(slot_page, start, per_section)
        order = jnp.argsort(jnp.where(owners == request, 0, 1), stable=True)[:MAX_PAGES].astype(jnp.int32)
        chosen = (order + start).astype(jnp.int32)
        block = cache[chosen].reshape(MAX_PAGES * PAGE, LAT + ROPE)
        mine = owners[order] == request
        position = numbers[order][:, None] * PAGE + offsets[None, :]
        valid = (mine[:, None] & (position < lengths[request])).reshape(-1)
        scores = jnp.dot(queries[request], block.T, preferred_element_type=jnp.float32) * scale
        scores = jnp.where(valid[None, :], scores, -1e30)
        highest = jnp.max(scores, axis=1, keepdims=True)
        weights = jnp.exp(scores - highest)
        denominator = jnp.sum(weights, axis=1, keepdims=True)
        summed = jnp.dot(weights.astype(jnp.bfloat16), block[:, :LAT], preferred_element_type=jnp.float32)
        return summed / denominator

    latent = lax.map(one_request, jnp.arange(BATCH).astype(jnp.int32))
    heads_out = jnp.einsum('bhl,hlv->bhv', latent.astype(jnp.float32), w_uv.astype(jnp.float32),
                           precision=lax.Precision.HIGHEST)
    heads_out = heads_out.astype(jnp.bfloat16).reshape(BATCH, HEADS * VDIM)
    projected = jnp.dot(heads_out, w_out, preferred_element_type=jnp.float32)
    return (hidden.astype(jnp.float32) + projected).astype(jnp.bfloat16)
```

```python
import functools

import jax
import jax.numpy as jnp
from jax import lax
from jax.experimental import pallas as pl
from jax.experimental.pallas import tpu as pltpu
from jax.sharding import PartitionSpec as P

ROPE = 64
NOPE = 128
LOWEST = -1e30
UNROLL = 4
AUX = 128
MIB = 1024 * 1024


def parts_of(value):
    high = value.astype(jnp.bfloat16).astype(jnp.float32)
    rest = value - high
    middle = rest.astype(jnp.bfloat16).astype(jnp.float32)
    return high, middle, rest - middle


def attend_kernel(
    owner_ref, page_ref, length_ref, query_ref, cache_ref, out_ref,
    pages, scores, high, denom, summed, packed, slots, owners, counts, sems,
):
    slot_count = cache_ref.shape[0]
    page_size = cache_ref.shape[2]
    requests, heads, _ = query_ref.shape
    latent = summed.shape[2]
    scale = (NOPE + ROPE) ** (-0.5)

    def copy(slot):
        return pltpu.make_async_copy(cache_ref.at[slot], pages.at[slot], sems.at[slot])

    def find(slot, found):
        owner = owner_ref[slot]

        @pl.when(owner >= 0)
        def _():
            copy(slot).start()
            mine = lax.rem(owner, requests)
            slots[found] = slot
            owners[found] = mine
            counts[found] = length_ref[mine] - page_ref[slot] * page_size

        return jnp.where(owner >= 0, found + 1, found)

    live = lax.fori_loop(0, slot_count, find, jnp.int32(0))
    blocks = lax.div(live + (UNROLL - 1), jnp.int32(UNROLL))

    high[...] = jnp.full(high.shape, LOWEST, jnp.float32)
    denom[...] = jnp.zeros(denom.shape, jnp.float32)
    summed[...] = jnp.zeros(summed.shape, jnp.float32)
    column = lax.broadcasted_iota(jnp.int32, (heads, page_size), 1)

    def score(block, carry):
        first = block * UNROLL
        for k in range(UNROLL):
            @pl.when(first + k < live)
            def _(k=k):
                copy(slots[first + k]).wait()
        for k in range(UNROLL):
            at = first + k
            entry = jnp.minimum(at, live - 1)
            mine = owners[entry]
            count = jnp.where(at < live, counts[entry], 0)
            found = jnp.dot(
                query_ref[mine], pages[slots[entry]], preferred_element_type=jnp.float32
            ) * scale
            found = jnp.where(column < count, found, LOWEST)
            scores[at] = found
            high[mine] = jnp.maximum(high[mine], found)
        return carry

    lax.fori_loop(0, blocks, score, 0)

    for mine in range(requests):
        top = jnp.max(high[mine], axis=1, keepdims=True)
        high[mine] = jnp.broadcast_to(top, (heads, page_size))

    def gather(block, carry):
        first = block * UNROLL
        for k in range(UNROLL):
            at = first + k
            entry = jnp.minimum(at, live - 1)
            mine = owners[entry]
            weights = jnp.exp(scores[at] - high[mine])
            weights = jnp.where(at < live, weights, 0.0)
            denom[mine] += weights
            summed[mine] += lax.dot_general(
                weights.astype(jnp.bfloat16),
                pages[slots[entry], :latent, :],
                (((1,), (1,)), ((), ())),
                preferred_element_type=jnp.float32,
            )
        return carry

    lax.fori_loop(0, blocks, gather, 0)

    lane = lax.broadcasted_iota(jnp.int32, (heads, AUX), 1)
    for mine in range(requests):
        packed[:, mine, :latent] = summed[mine]
        total = jnp.broadcast_to(jnp.sum(denom[mine], axis=1, keepdims=True), (heads, AUX))
        aux = jnp.zeros((heads, AUX), jnp.float32)
        for k, part in enumerate(parts_of(high[mine]) + parts_of(total)):
            aux = jnp.where(lane == k, part, aux)
        packed[:, mine, latent:] = aux
    out_ref[...] = packed[...].reshape(out_ref.shape).astype(jnp.bfloat16)


def attend(queries, cache, slot_request, slot_page, lengths, latent):
    requests, heads, width = queries.shape
    slot_count, page_size, _ = cache.shape
    padded = slot_count + UNROLL
    smem = pl.BlockSpec(memory_space=pltpu.SMEM)
    vmem = pl.BlockSpec(memory_space=pltpu.VMEM)
    return pl.pallas_call(
        attend_kernel,
        out_shape=jax.ShapeDtypeStruct((heads * requests, latent + AUX), jnp.bfloat16),
        in_specs=[smem, smem, smem, vmem, pl.BlockSpec(memory_space=pl.ANY)],
        out_specs=vmem,
        scratch_shapes=[
            pltpu.VMEM((slot_count, width, page_size), jnp.bfloat16),
            pltpu.VMEM((padded, heads, page_size), jnp.float32),
            pltpu.VMEM((requests, heads, page_size), jnp.float32),
            pltpu.VMEM((requests, heads, page_size), jnp.float32),
            pltpu.VMEM((requests, heads, latent), jnp.float32),
            pltpu.VMEM((heads, requests, latent + AUX), jnp.float32),
            pltpu.SMEM((padded,), jnp.int32),
            pltpu.SMEM((padded,), jnp.int32),
            pltpu.SMEM((padded,), jnp.int32),
            pltpu.SemaphoreType.DMA((slot_count,)),
        ],
        compiler_params=pltpu.CompilerParams(vmem_limit_bytes=40 * MIB),
        name="attend",
    )(slot_request, slot_page, lengths, queries, jnp.swapaxes(cache, 1, 2))


def value_kernel(copies, part_ref, weight_ref, out_ref, weight, sem):
    latent = weight.shape[0]
    sources = weight_ref.shape[0]
    requests = part_ref.shape[0] // sources
    fetch = pltpu.make_async_copy(weight_ref.at[lax.axis_index("kv")], weight, sem)
    fetch.start()
    aux = part_ref[:, latent:].astype(jnp.float32)
    high = (aux[:, 0:1] + aux[:, 1:2] + aux[:, 2:3]).reshape(sources, requests, 1)
    denom = (aux[:, 3:4] + aux[:, 4:5] + aux[:, 5:6]).reshape(sources, requests, 1)
    factor = jnp.exp(high - jnp.max(high, axis=0, keepdims=True))
    total = jnp.sum(denom * factor, axis=0)
    parts = part_ref[:, :latent].astype(jnp.float32).reshape(sources, requests, latent)
    finished = jnp.sum(parts * factor, axis=0) / total
    rows = jnp.concatenate(parts_of(finished), axis=0).astype(jnp.bfloat16)
    fetch.wait()
    product = jnp.dot(rows, weight[...], preferred_element_type=jnp.float32)
    value = product[:requests] + product[requests : 2 * requests] + product[2 * requests :]
    value = jnp.concatenate([value] * copies, axis=0)
    out_ref[...] = value.astype(jnp.bfloat16)


def value_project(parts, w_uv, copies):
    heads, latent, value_width = w_uv.shape
    requests = parts.shape[0] // heads
    vmem = pl.BlockSpec(memory_space=pltpu.VMEM)
    return pl.pallas_call(
        functools.partial(value_kernel, copies),
        out_shape=jax.ShapeDtypeStruct((copies * requests, value_width), jnp.bfloat16),
        in_specs=[vmem, pl.BlockSpec(memory_space=pl.ANY)],
        out_specs=vmem,
        scratch_shapes=[
            pltpu.VMEM((latent, value_width), jnp.bfloat16),
            pltpu.SemaphoreType.DMA(()),
        ],
        compiler_params=pltpu.CompilerParams(vmem_limit_bytes=16 * MIB),
        name="value_project",
    )(parts, w_uv)


def body(queries, cache, slot_request, slot_page, lengths, w_uv, w_out, hidden):
    requests, heads, _ = queries.shape
    latent, value_width = w_uv.shape[1:]
    sections = lax.axis_size("section")
    sources = lax.axis_size("kv")
    groups = lax.axis_size("head")
    parts = attend(queries, cache, slot_request, slot_page, lengths, latent)
    parts = lax.all_to_all(parts, "kv", 0, 0, tiled=True)
    values = value_project(parts, w_uv, sections * sources)
    values = lax.all_to_all(values, ("section", "kv"), 0, 0, tiled=True)
    values = values.reshape(sections, sources, requests, value_width)
    values = values.transpose(0, 2, 1, 3).reshape(sections * requests, heads * value_width)
    projected = jnp.dot(values, w_out, preferred_element_type=jnp.float32)
    total = projected
    for step in (2, 1, 3):
        total = total + lax.ppermute(
            projected, "head", [(k, (k + step) % groups) for k in range(groups)]
        )
    return (hidden.astype(jnp.float32) + total).astype(jnp.bfloat16)


def solution(mesh):
    placed = (
        P("section", "head", None),
        P(("section", "kv"), None, None),
        P(("section", "kv")),
        P(("section", "kv")),
        P("section"),
        P("head", None, None),
        P("head", ("section", "kv")),
        P(None, ("section", "kv")),
    )
    return jax.shard_map(
        body, mesh=mesh, in_specs=placed, out_specs=P(None, ("section", "kv")), check_vma=False
    )
```

```python
import functools

import jax
import jax.numpy as jnp
from jax import lax
from jax.experimental import pallas as pl
from jax.experimental.pallas import tpu as pltpu
from jax.sharding import PartitionSpec as P

ROPE = 64
NOPE = 128
LOWEST = -1e30
UNROLL = 8
AHEAD = 4
SCAN = 16
AUX = 128
MIB = 1024 * 1024


def parts_of(value):
    high = value.astype(jnp.bfloat16).astype(jnp.float32)
    rest = value - high
    middle = rest.astype(jnp.bfloat16).astype(jnp.float32)
    return high, middle, rest - middle


def attend_kernel(
    owner_hbm, page_hbm, length_hbm, query_hbm, cache_ref, out_ref,
    pages, scores, high, denom, summed, packed, query_ref, owner_ref, page_ref, length_ref,
    slots, sems, few,
):
    slot_count = cache_ref.shape[0]
    page_size = cache_ref.shape[2]
    requests, heads, _ = query_ref.shape
    latent = summed.shape[2]
    scale = (NOPE + ROPE) ** (-0.5)
    fetches = [
        pltpu.make_async_copy(source, target, few.at[k])
        for k, (source, target) in enumerate(
            (
                (owner_hbm, owner_ref),
                (page_hbm, page_ref),
                (length_hbm, length_ref),
                (query_hbm, query_ref),
            )
        )
    ]
    for fetch in fetches:
        fetch.start()

    high[...] = jnp.full(high.shape, LOWEST, jnp.float32)
    denom[...] = jnp.zeros(denom.shape, jnp.float32)
    summed[...] = jnp.zeros(summed.shape, jnp.float32)
    for fetch in fetches[:3]:
        fetch.wait()

    def note(slot, found):
        alive = owner_ref[slot] >= 0
        slots[jnp.where(alive, found, slot_count - 1 - slot + found)] = slot
        return jnp.where(alive, found + 1, found)

    live = lax.fori_loop(0, slot_count, note, jnp.int32(0), unroll=SCAN)
    blocks = lax.div(live + (UNROLL - 1), jnp.int32(UNROLL))

    def fetch_block(block):
        for k in range(UNROLL):
            pltpu.make_async_copy(
                cache_ref.at[slots[block * UNROLL + k]],
                pages.at[block * UNROLL + k],
                sems.at[block],
            ).start()

    def ahead(block, carry):
        fetch_block(block)
        return carry

    lax.fori_loop(0, jnp.minimum(blocks, AHEAD), ahead, 0)

    column = lax.broadcasted_iota(jnp.int32, (heads, page_size), 1)

    def entry_of(at):
        slot = slots[at]
        return slot, lax.rem(jnp.maximum(owner_ref[slot], 0), requests)

    def score(block, carry):
        first = block * UNROLL

        @pl.when(block + AHEAD < blocks)
        def _():
            fetch_block(block + AHEAD)

        pltpu.make_async_copy(
            cache_ref.at[pl.ds(0, UNROLL)], pages.at[pl.ds(first, UNROLL)], sems.at[block]
        ).wait()

        def keep(at, slot, mine, found):
            count = jnp.where(at < live, length_ref[mine] - page_ref[slot] * page_size, 0)
            found = jnp.where(column < count, found * scale, LOWEST)
            scores[at] = found
            high[mine] = jnp.maximum(high[mine], found)

        for k in range(UNROLL):
            slot, mine = entry_of(first + k)
            keep(first + k, slot, mine, jnp.dot(
                query_ref[mine], pages[first + k], preferred_element_type=jnp.float32
            ))
        return carry

    fetches[3].wait()
    lax.fori_loop(0, blocks, score, 0)

    for mine in range(requests):
        top = jnp.max(high[mine], axis=1, keepdims=True)
        high[mine] = jnp.broadcast_to(top, (heads, page_size))

    def weigh(at):
        slot, mine = entry_of(at)
        weights = jnp.exp(scores[at] - high[mine])
        weights = jnp.where(at < live, weights, 0.0)
        denom[mine] += weights
        return slot, mine, weights.astype(jnp.bfloat16)

    def gather(block, carry):
        first = block * UNROLL
        for k in range(0, UNROLL, 2):
            sa, ma, wa = weigh(first + k)
            sb, mb, wb = weigh(first + k + 1)
            zero = jnp.zeros_like(wa)
            lhs = jnp.concatenate([jnp.concatenate([wa, zero], axis=1), jnp.concatenate([zero, wb], axis=1)], axis=0)
            rhs = jnp.concatenate([pages[first + k, :latent, :], pages[first + k + 1, :latent, :]], axis=1)
            both = lax.dot_general(lhs, rhs, (((1,), (1,)), ((), ())), preferred_element_type=jnp.float32)
            summed[ma] += both[:heads]
            summed[mb] += both[heads:]
        return carry

    lax.fori_loop(0, blocks, gather, 0)

    lane = lax.broadcasted_iota(jnp.int32, (heads, AUX), 1)
    for mine in range(requests):
        packed[:, mine, :latent] = summed[mine]
        total = jnp.broadcast_to(jnp.sum(denom[mine], axis=1, keepdims=True), (heads, AUX))
        aux = jnp.zeros((heads, AUX), jnp.float32)
        for k, part in enumerate(parts_of(high[mine]) + parts_of(total)):
            aux = jnp.where(lane == k, part, aux)
        packed[:, mine, latent:] = aux
    out_ref[...] = packed[...].reshape(out_ref.shape).astype(jnp.bfloat16)


def attend(queries, cache, slot_request, slot_page, lengths, latent):
    requests, heads, width = queries.shape
    slot_count, page_size, _ = cache.shape
    padded = slot_count + UNROLL
    vmem = pl.BlockSpec(memory_space=pltpu.VMEM)
    return pl.pallas_call(
        attend_kernel,
        out_shape=jax.ShapeDtypeStruct((heads * requests, latent + AUX), jnp.bfloat16),
        in_specs=[pl.BlockSpec(memory_space=pltpu.HBM)] * 5,
        out_specs=vmem,
        scratch_shapes=[
            pltpu.VMEM((slot_count, width, page_size), jnp.bfloat16),
            pltpu.VMEM((padded, heads, page_size), jnp.float32),
            pltpu.VMEM((requests, heads, page_size), jnp.float32),
            pltpu.VMEM((requests, heads, page_size), jnp.float32),
            pltpu.VMEM((requests, heads, latent), jnp.float32),
            pltpu.VMEM((heads, requests, latent + AUX), jnp.float32),
            pltpu.VMEM(queries.shape, queries.dtype),
            pltpu.SMEM(slot_request.shape, jnp.int32),
            pltpu.SMEM(slot_page.shape, jnp.int32),
            pltpu.SMEM(lengths.shape, jnp.int32),
            pltpu.SMEM((padded,), jnp.int32),
            pltpu.SemaphoreType.DMA((slot_count // UNROLL,)),
            pltpu.SemaphoreType.DMA((4,)),
        ],
        compiler_params=pltpu.CompilerParams(vmem_limit_bytes=62 * MIB),
        name="attend",
    )(slot_request, slot_page, lengths, queries, jnp.swapaxes(cache, 1, 2))


def value_kernel(copies, part_ref, weight_ref, out_ref, weight, sem):
    latent = weight.shape[0]
    sources = weight_ref.shape[0]
    requests = part_ref.shape[0] // sources
    fetch = pltpu.make_async_copy(weight_ref.at[lax.axis_index("kv")], weight, sem)
    fetch.start()
    aux = part_ref[:, latent:].astype(jnp.float32)
    high = (aux[:, 0:1] + aux[:, 1:2] + aux[:, 2:3]).reshape(sources, requests, 1)
    denom = (aux[:, 3:4] + aux[:, 4:5] + aux[:, 5:6]).reshape(sources, requests, 1)
    factor = jnp.exp(high - jnp.max(high, axis=0, keepdims=True))
    total = jnp.sum(denom * factor, axis=0)
    parts = part_ref[:, :latent].astype(jnp.float32).reshape(sources, requests, latent)
    finished = jnp.sum(parts * factor, axis=0) / total
    rows = jnp.concatenate(parts_of(finished), axis=0).astype(jnp.bfloat16)
    fetch.wait()
    product = jnp.dot(rows, weight[...], preferred_element_type=jnp.float32)
    value = product[:requests] + product[requests : 2 * requests] + product[2 * requests :]
    value = jnp.concatenate([value] * copies, axis=0)
    out_ref[...] = value.astype(jnp.bfloat16)


def value_project(parts, w_uv, copies):
    heads, latent, value_width = w_uv.shape
    requests = parts.shape[0] // heads
    vmem = pl.BlockSpec(memory_space=pltpu.VMEM)
    return pl.pallas_call(
        functools.partial(value_kernel, copies),
        out_shape=jax.ShapeDtypeStruct((copies * requests, value_width), jnp.bfloat16),
        in_specs=[vmem, pl.BlockSpec(memory_space=pl.ANY)],
        out_specs=vmem,
        scratch_shapes=[
            pltpu.VMEM((latent, value_width), jnp.bfloat16),
            pltpu.SemaphoreType.DMA(()),
        ],
        compiler_params=pltpu.CompilerParams(vmem_limit_bytes=61 * MIB),
        name="value_project",
    )(parts, w_uv)


def body(queries, cache, slot_request, slot_page, lengths, w_uv, w_out, hidden):
    requests, heads, _ = queries.shape
    latent, value_width = w_uv.shape[1:]
    sections = lax.axis_size("section")
    sources = lax.axis_size("kv")
    groups = lax.axis_size("head")
    parts = attend(queries, cache, slot_request, slot_page, lengths, latent)
    parts = lax.all_to_all(parts, "kv", 0, 0, tiled=True)
    values = value_project(parts, w_uv, sections * sources)
    values = lax.all_to_all(values, ("section", "kv"), 0, 0, tiled=True)
    values = values.reshape(sections, sources, requests, value_width)
    values = values.transpose(0, 2, 1, 3).reshape(sections * requests, heads * value_width)
    projected = jnp.dot(values, w_out, preferred_element_type=jnp.float32)
    total = projected
    for step in (2, 1, 3):
        total = total + lax.ppermute(
            projected, "head", [(k, (k + step) % groups) for k in range(groups)]
        )
    return (hidden.astype(jnp.float32) + total).astype(jnp.bfloat16)


def solution(mesh):
    placed = (
        P("section", "head", None),
        P(("section", "kv"), None, None),
        P(("section", "kv")),
        P(("section", "kv")),
        P("section"),
        P("head", None, None),
        P("head", ("section", "kv")),
        P(None, ("section", "kv")),
    )
    return jax.shard_map(
        body, mesh=mesh, in_specs=placed, out_specs=P(None, ("section", "kv")), check_vma=False
    )
```

```python
import functools

import jax
import jax.numpy as jnp
from jax import lax
from jax.experimental import pallas as pl
from jax.experimental.pallas import tpu as pltpu
from jax.sharding import PartitionSpec as P

ROPE = 64
NOPE = 128
LOWEST = -1e30
UNROLL = 8
AHEAD = 4
SCAN = 16
BLIND = 16
AUX = 128
MIB = 1024 * 1024


def parts_of(value):
    high = value.astype(jnp.bfloat16).astype(jnp.float32)
    rest = value - high
    middle = rest.astype(jnp.bfloat16).astype(jnp.float32)
    return high, middle, rest - middle


def attend_kernel(
    owner_hbm, page_hbm, length_hbm, query_hbm, cache_ref, weight_hbm, out_ref, weight_ref,
    pages, scores, high, denom, summed, packed, query_ref, owner_ref, page_ref, length_ref,
    slots, sems, few,
):
    slot_count = cache_ref.shape[0]
    page_size = cache_ref.shape[2]
    requests, heads, _ = query_ref.shape
    latent = summed.shape[2]
    scale = (NOPE + ROPE) ** (-0.5)
    fetches = [
        pltpu.make_async_copy(source, target, few.at[k])
        for k, (source, target) in enumerate(
            (
                (owner_hbm, owner_ref),
                (page_hbm, page_ref),
                (length_hbm, length_ref),
                (query_hbm, query_ref),
                (weight_hbm.at[lax.axis_index("kv")], weight_ref),
            )
        )
    ]
    for fetch in fetches:
        fetch.start()

    def blind(part):
        span = pl.ds(part * UNROLL, UNROLL)
        return pltpu.make_async_copy(cache_ref.at[span], pages.at[span], sems.at[part])

    early = BLIND // UNROLL
    for part in range(early):
        blind(part).start()

    high[...] = jnp.full(high.shape, LOWEST, jnp.float32)
    denom[...] = jnp.zeros(denom.shape, jnp.float32)
    summed[...] = jnp.zeros(summed.shape, jnp.float32)
    for fetch in fetches[:3]:
        fetch.wait()

    def note(slot, found):
        alive = owner_ref[slot] >= 0
        slots[jnp.where(alive, found, slot_count - 1 - slot + found)] = slot
        return jnp.where(alive, found + 1, found)

    for k in range(UNROLL):
        slots[slot_count + k] = 0
    here = lax.fori_loop(0, BLIND, note, jnp.int32(0), unroll=SCAN)
    live = lax.fori_loop(BLIND, slot_count, note, here, unroll=SCAN)
    blocks = lax.div(live + (UNROLL - 1), jnp.int32(UNROLL))
    batches = lax.div(live - here + (UNROLL - 1), jnp.int32(UNROLL))

    def fetch_batch(batch):
        for k in range(UNROLL):
            pltpu.make_async_copy(
                cache_ref.at[slots[here + batch * UNROLL + k]],
                pages.at[BLIND + batch * UNROLL + k],
                sems.at[early + batch],
            ).start()

    def ahead(batch, carry):
        fetch_batch(batch)
        return carry

    lax.fori_loop(0, jnp.minimum(batches, AHEAD), ahead, 0)

    column = lax.broadcasted_iota(jnp.int32, (heads, page_size), 1)

    def entry_of(at):
        slot = slots[at]
        place = jnp.where(at < here, slot, BLIND - here + at)
        place = jnp.where(at < live, place, 0)
        return slot, place, lax.rem(jnp.maximum(owner_ref[slot], 0), requests)

    def arrive(batch, carry):
        @pl.when(batch + AHEAD < batches)
        def _():
            fetch_batch(batch + AHEAD)

        span = pl.ds(BLIND + batch * UNROLL, UNROLL)
        pltpu.make_async_copy(
            cache_ref.at[pl.ds(0, UNROLL)], pages.at[span], sems.at[early + batch]
        ).wait()
        return carry

    def score(block, arrived):
        first = block * UNROLL
        needed = lax.div(first + (2 * UNROLL - 1) - here, jnp.int32(UNROLL))
        needed = jnp.clip(needed, arrived, batches)
        lax.fori_loop(arrived, needed, arrive, 0)

        def keep(at, slot, mine, found):
            count = jnp.where(at < live, length_ref[mine] - page_ref[slot] * page_size, 0)
            found = jnp.where(column < count, found * scale, LOWEST)
            scores[at] = found
            high[mine] = jnp.maximum(high[mine], found)

        for k in range(UNROLL):
            slot, place, mine = entry_of(first + k)
            keep(first + k, slot, mine, jnp.dot(
                query_ref[mine], pages[place], preferred_element_type=jnp.float32
            ))
        return needed

    fetches[3].wait()
    for part in range(early):
        blind(part).wait()
    lax.fori_loop(0, blocks, score, jnp.int32(0))

    for mine in range(requests):
        top = jnp.max(high[mine], axis=1, keepdims=True)
        high[mine] = jnp.broadcast_to(top, (heads, page_size))

    def weigh(at):
        slot, place, mine = entry_of(at)
        weights = jnp.exp(scores[at] - high[mine])
        weights = jnp.where(at < live, weights, 0.0)
        denom[mine] += weights
        return place, mine, weights.astype(jnp.bfloat16)

    def gather(block, carry):
        first = block * UNROLL
        for k in range(0, UNROLL, 2):
            sa, ma, wa = weigh(first + k)
            sb, mb, wb = weigh(first + k + 1)
            zero = jnp.zeros_like(wa)
            lhs = jnp.concatenate([jnp.concatenate([wa, zero], axis=1), jnp.concatenate([zero, wb], axis=1)], axis=0)
            rhs = jnp.concatenate([pages[sa, :latent, :], pages[sb, :latent, :]], axis=1)
            both = lax.dot_general(lhs, rhs, (((1,), (1,)), ((), ())), preferred_element_type=jnp.float32)
            summed[ma] += both[:heads]
            summed[mb] += both[heads:]
        return carry

    lax.fori_loop(0, blocks, gather, 0)

    lane = lax.broadcasted_iota(jnp.int32, (heads, AUX), 1)
    for mine in range(requests):
        packed[:, mine, :latent] = summed[mine]
        total = jnp.broadcast_to(jnp.sum(denom[mine], axis=1, keepdims=True), (heads, AUX))
        aux = jnp.zeros((heads, AUX), jnp.float32)
        for k, part in enumerate(parts_of(high[mine]) + parts_of(total)):
            aux = jnp.where(lane == k, part, aux)
        packed[:, mine, latent:] = aux
    fetches[4].wait()
    out_ref[...] = packed[...].reshape(out_ref.shape).astype(jnp.bfloat16)


def attend(queries, cache, slot_request, slot_page, lengths, w_uv):
    requests, heads, width = queries.shape
    slot_count, page_size, _ = cache.shape
    padded = slot_count + UNROLL
    latent = w_uv.shape[1]
    operands = (slot_request, slot_page, lengths, queries, jnp.swapaxes(cache, 1, 2), w_uv)
    operands = [pltpu.with_memory_space_constraint(k, pltpu.HBM) for k in operands]
    vmem = pl.BlockSpec(memory_space=pltpu.VMEM)
    return pl.pallas_call(
        attend_kernel,
        out_shape=(
            jax.ShapeDtypeStruct((heads * requests, latent + AUX), jnp.bfloat16),
            jax.ShapeDtypeStruct(w_uv.shape[1:], w_uv.dtype),
        ),
        in_specs=[pl.BlockSpec(memory_space=pltpu.HBM)] * len(operands),
        out_specs=(vmem, vmem),
        scratch_shapes=[
            pltpu.VMEM((slot_count, width, page_size), jnp.bfloat16),
            pltpu.VMEM((padded, heads, page_size), jnp.float32),
            pltpu.VMEM((requests, heads, page_size), jnp.float32),
            pltpu.VMEM((requests, heads, page_size), jnp.float32),
            pltpu.VMEM((requests, heads, latent), jnp.float32),
            pltpu.VMEM((heads, requests, latent + AUX), jnp.float32),
            pltpu.VMEM(queries.shape, queries.dtype),
            pltpu.SMEM(slot_request.shape, jnp.int32),
            pltpu.SMEM(slot_page.shape, jnp.int32),
            pltpu.SMEM(lengths.shape, jnp.int32),
            pltpu.SMEM((padded,), jnp.int32),
            pltpu.SemaphoreType.DMA((padded // UNROLL,)),
            pltpu.SemaphoreType.DMA((len(operands) - 1,)),
        ],
        compiler_params=pltpu.CompilerParams(vmem_limit_bytes=24 * MIB),
        name="attend",
    )(*operands)


def value_kernel(copies, part_ref, weight_ref, out_ref):
    latent = weight_ref.shape[0]
    requests = out_ref.shape[0] // copies
    sources = part_ref.shape[0] // requests
    aux = part_ref[:, latent:].astype(jnp.float32)
    high = (aux[:, 0:1] + aux[:, 1:2] + aux[:, 2:3]).reshape(sources, requests, 1)
    denom = (aux[:, 3:4] + aux[:, 4:5] + aux[:, 5:6]).reshape(sources, requests, 1)
    factor = jnp.exp(high - jnp.max(high, axis=0, keepdims=True))
    total = jnp.sum(denom * factor, axis=0)
    parts = part_ref[:, :latent].astype(jnp.float32).reshape(sources, requests, latent)
    finished = jnp.sum(parts * factor, axis=0) / total
    rows = jnp.concatenate(parts_of(finished), axis=0).astype(jnp.bfloat16)
    product = jnp.dot(rows, weight_ref[...], preferred_element_type=jnp.float32)
    value = product[:requests] + product[requests : 2 * requests] + product[2 * requests :]
    value = jnp.concatenate([value] * copies, axis=0)
    out_ref[...] = value.astype(jnp.bfloat16)


def value_project(parts, weight, requests, copies):
    vmem = pl.BlockSpec(memory_space=pltpu.VMEM)
    return pl.pallas_call(
        functools.partial(value_kernel, copies),
        out_shape=jax.ShapeDtypeStruct((copies * requests, weight.shape[1]), jnp.bfloat16),
        in_specs=[vmem, vmem],
        out_specs=vmem,
        compiler_params=pltpu.CompilerParams(vmem_limit_bytes=16 * MIB),
        name="value_project",
    )(parts, weight)


def body(queries, cache, slot_request, slot_page, lengths, w_uv, w_out, hidden):
    requests, heads, _ = queries.shape
    value_width = w_uv.shape[2]
    sections = lax.axis_size("section")
    sources = lax.axis_size("kv")
    groups = lax.axis_size("head")
    parts, weight = attend(queries, cache, slot_request, slot_page, lengths, w_uv)
    parts = lax.all_to_all(parts, "kv", 0, 0, tiled=True)
    values = value_project(parts, weight, requests, sections * sources)
    values = lax.all_to_all(values, ("section", "kv"), 0, 0, tiled=True)
    values = values.reshape(sections, sources, requests, value_width)
    values = values.transpose(0, 2, 1, 3).reshape(sections * requests, heads * value_width)
    projected = jnp.dot(values, w_out, preferred_element_type=jnp.float32)
    total = projected
    for step in (2, 1, 3):
        total = total + lax.ppermute(
            projected, "head", [(k, (k + step) % groups) for k in range(groups)]
        )
    return (hidden.astype(jnp.float32) + total).astype(jnp.bfloat16)


def solution(mesh):
    placed = (
        P("section", "head", None),
        P(("section", "kv"), None, None),
        P(("section", "kv")),
        P(("section", "kv")),
        P("section"),
        P("head", None, None),
        P("head", ("section", "kv")),
        P(None, ("section", "kv")),
    )
    return jax.shard_map(
        body, mesh=mesh, in_specs=placed, out_specs=P(None, ("section", "kv")), check_vma=False
    )
```

```python
import functools

import jax
import jax.numpy as jnp
from jax import lax
from jax.experimental import pallas as pl
from jax.experimental.pallas import tpu as pltpu
from jax.sharding import PartitionSpec as P

ROPE = 64
NOPE = 128
LOWEST = -1e30
UNROLL = 8
AHEAD = 4
SCAN = 16
BLIND = 16
GROUP = 16
AUX = 128
MIB = 1024 * 1024


def parts_of(value):
    high = value.astype(jnp.bfloat16).astype(jnp.float32)
    rest = value - high
    middle = rest.astype(jnp.bfloat16).astype(jnp.float32)
    return high, middle, rest - middle


def attend_kernel(
    owner_hbm, page_hbm, length_hbm, query_hbm, cache_ref, weight_hbm, out_ref,
    pages, scores, high, denom, summed, packed, values, query_ref, owner_ref, page_ref, length_ref,
    weight_ref, slots, sems, few,
):
    slot_count = cache_ref.shape[0]
    page_size = cache_ref.shape[2]
    requests, heads, _ = query_ref.shape
    latent = summed.shape[2]
    scale = (NOPE + ROPE) ** (-0.5)
    fetches = [
        pltpu.make_async_copy(source, target, few.at[k])
        for k, (source, target) in enumerate(
            (
                (owner_hbm, owner_ref),
                (page_hbm, page_ref),
                (length_hbm, length_ref),
                (query_hbm, query_ref),
                (weight_hbm, weight_ref),
            )
        )
    ]
    for fetch in fetches[:4]:
        fetch.start()

    def blind(part):
        span = pl.ds(part * UNROLL, UNROLL)
        return pltpu.make_async_copy(cache_ref.at[span], pages.at[span], sems.at[part])

    early = BLIND // UNROLL
    for part in range(early):
        blind(part).start()

    high[...] = jnp.full(high.shape, LOWEST, jnp.float32)
    denom[...] = jnp.zeros(denom.shape, jnp.float32)
    summed[...] = jnp.zeros(summed.shape, jnp.float32)
    for fetch in fetches[:3]:
        fetch.wait()

    def note(slot, found):
        alive = owner_ref[slot] >= 0
        slots[jnp.where(alive, found, slot_count - 1 - slot + found)] = slot
        return jnp.where(alive, found + 1, found)

    for k in range(UNROLL):
        slots[slot_count + k] = 0
    here = lax.fori_loop(0, BLIND, note, jnp.int32(0), unroll=SCAN)
    live = lax.fori_loop(BLIND, slot_count, note, here, unroll=SCAN)
    blocks = lax.div(live + (UNROLL - 1), jnp.int32(UNROLL))
    batches = lax.div(live - here + (UNROLL - 1), jnp.int32(UNROLL))

    def fetch_batch(batch):
        for k in range(UNROLL):
            pltpu.make_async_copy(
                cache_ref.at[slots[here + batch * UNROLL + k]],
                pages.at[BLIND + batch * UNROLL + k],
                sems.at[early + batch],
            ).start()

    def ahead(batch, carry):
        fetch_batch(batch)
        return carry

    lax.fori_loop(0, jnp.minimum(batches, AHEAD), ahead, 0)

    column = lax.broadcasted_iota(jnp.int32, (heads, page_size), 1)

    def entry_of(at):
        slot = slots[at]
        place = jnp.where(at < here, slot, BLIND - here + at)
        place = jnp.where(at < live, place, 0)
        return slot, place, lax.rem(jnp.maximum(owner_ref[slot], 0), requests)

    def arrive(batch, carry):
        @pl.when(batch + AHEAD < batches)
        def _():
            fetch_batch(batch + AHEAD)

        span = pl.ds(BLIND + batch * UNROLL, UNROLL)
        pltpu.make_async_copy(
            cache_ref.at[pl.ds(0, UNROLL)], pages.at[span], sems.at[early + batch]
        ).wait()
        return carry

    def score(block, arrived):
        first = block * UNROLL
        needed = lax.div(first + (2 * UNROLL - 1) - here, jnp.int32(UNROLL))
        needed = jnp.clip(needed, arrived, batches)
        lax.fori_loop(arrived, needed, arrive, 0)

        def keep(at, slot, mine, found):
            count = jnp.where(at < live, length_ref[mine] - page_ref[slot] * page_size, 0)
            found = jnp.where(column < count, found * scale, LOWEST)
            scores[at] = found
            high[mine] = jnp.maximum(high[mine], found)

        for k in range(UNROLL):
            slot, place, mine = entry_of(first + k)
            keep(first + k, slot, mine, jnp.dot(
                query_ref[mine], pages[place], preferred_element_type=jnp.float32
            ))
        return needed

    fetches[3].wait()
    for part in range(early):
        blind(part).wait()
    lax.fori_loop(0, blocks, score, jnp.int32(0))
    fetches[4].start()

    for mine in range(requests):
        top = jnp.max(high[mine], axis=1, keepdims=True)
        high[mine] = jnp.broadcast_to(top, (heads, page_size))

    def weigh(at):
        slot, place, mine = entry_of(at)
        weights = jnp.exp(scores[at] - high[mine])
        weights = jnp.where(at < live, weights, 0.0)
        denom[mine] += weights
        return place, mine, weights.astype(jnp.bfloat16)

    def gather(block, carry):
        first = block * UNROLL
        for k in range(0, UNROLL, 2):
            sa, ma, wa = weigh(first + k)
            sb, mb, wb = weigh(first + k + 1)
            zero = jnp.zeros_like(wa)
            lhs = jnp.concatenate([jnp.concatenate([wa, zero], axis=1), jnp.concatenate([zero, wb], axis=1)], axis=0)
            rhs = jnp.concatenate([pages[sa, :latent, :], pages[sb, :latent, :]], axis=1)
            both = lax.dot_general(lhs, rhs, (((1,), (1,)), ((), ())), preferred_element_type=jnp.float32)
            summed[ma] += both[:heads]
            summed[mb] += both[heads:]
        return carry

    lax.fori_loop(0, blocks, gather, 0)

    lane = lax.broadcasted_iota(jnp.int32, (heads, AUX), 1)
    width = weight_ref.shape[2]
    for mine in range(requests):
        packed[:, mine, :] = summed[mine]
        total = jnp.broadcast_to(jnp.sum(denom[mine], axis=1, keepdims=True), (heads, AUX))
        aux = jnp.zeros((heads, AUX), jnp.float32)
        for k, part in enumerate(parts_of(high[mine]) + parts_of(total)):
            aux = jnp.where(lane == k, part, aux)
        values[:, mine, width:] = aux
    fetches[4].wait()

    def project(block, carry):
        for k in range(GROUP):
            head = block * GROUP + k
            rows = jnp.concatenate(parts_of(packed[head]), axis=0).astype(jnp.bfloat16)
            product = jnp.dot(rows, weight_ref[head], preferred_element_type=jnp.float32)
            values[head, :, :width] = (
                product[:requests] + product[requests : 2 * requests] + product[2 * requests :]
            )
        return carry

    lax.fori_loop(0, heads // GROUP, project, 0)
    out_ref[...] = values[...].reshape(out_ref.shape).astype(jnp.bfloat16)


def attend(queries, cache, slot_request, slot_page, lengths, w_uv):
    requests, heads, width = queries.shape
    slot_count, page_size, _ = cache.shape
    padded = slot_count + UNROLL
    latent = w_uv.shape[1]
    operands = (slot_request, slot_page, lengths, queries, jnp.swapaxes(cache, 1, 2), w_uv)
    operands = [pltpu.with_memory_space_constraint(k, pltpu.HBM) for k in operands]
    vmem = pl.BlockSpec(memory_space=pltpu.VMEM)
    return pl.pallas_call(
        attend_kernel,
        out_shape=jax.ShapeDtypeStruct((heads * requests, w_uv.shape[2] + AUX), jnp.bfloat16),
        in_specs=[pl.BlockSpec(memory_space=pltpu.HBM)] * len(operands),
        out_specs=vmem,
        scratch_shapes=[
            pltpu.VMEM((slot_count, width, page_size), jnp.bfloat16),
            pltpu.VMEM((padded, heads, page_size), jnp.float32),
            pltpu.VMEM((requests, heads, page_size), jnp.float32),
            pltpu.VMEM((requests, heads, page_size), jnp.float32),
            pltpu.VMEM((requests, heads, latent), jnp.float32),
            pltpu.VMEM((heads, requests, latent), jnp.float32),
            pltpu.VMEM((heads, requests, w_uv.shape[2] + AUX), jnp.float32),
            pltpu.VMEM(queries.shape, queries.dtype),
            pltpu.SMEM(slot_request.shape, jnp.int32),
            pltpu.SMEM(slot_page.shape, jnp.int32),
            pltpu.SMEM(lengths.shape, jnp.int32),
            pltpu.VMEM(w_uv.shape, w_uv.dtype),
            pltpu.SMEM((padded,), jnp.int32),
            pltpu.SemaphoreType.DMA((padded // UNROLL,)),
            pltpu.SemaphoreType.DMA((len(operands) - 1,)),
        ],
        compiler_params=pltpu.CompilerParams(vmem_limit_bytes=28 * MIB),
        name="attend",
    )(*operands)


def combine_kernel(copies, part_ref, out_ref):
    width = out_ref.shape[1]
    requests = out_ref.shape[0] // copies
    sources = part_ref.shape[0] // requests
    aux = part_ref[:, width:].astype(jnp.float32)
    high = (aux[:, 0:1] + aux[:, 1:2] + aux[:, 2:3]).reshape(sources, requests, 1)
    denom = (aux[:, 3:4] + aux[:, 4:5] + aux[:, 5:6]).reshape(sources, requests, 1)
    factor = jnp.exp(high - jnp.max(high, axis=0, keepdims=True))
    total = jnp.sum(denom * factor, axis=0)
    parts = part_ref[:, :width].astype(jnp.float32).reshape(sources, requests, width)
    value = jnp.sum(parts * factor, axis=0) / total
    value = jnp.concatenate([value] * copies, axis=0)
    out_ref[...] = value.astype(jnp.bfloat16)


def combine(parts, requests, width, copies):
    vmem = pl.BlockSpec(memory_space=pltpu.VMEM)
    return pl.pallas_call(
        functools.partial(combine_kernel, copies),
        out_shape=jax.ShapeDtypeStruct((copies * requests, width), jnp.bfloat16),
        in_specs=[vmem],
        out_specs=vmem,
        compiler_params=pltpu.CompilerParams(vmem_limit_bytes=16 * MIB),
        name="combine",
    )(parts)


def body(queries, cache, slot_request, slot_page, lengths, w_uv, w_out, hidden):
    requests, heads, _ = queries.shape
    value_width = w_uv.shape[2]
    sections = lax.axis_size("section")
    sources = lax.axis_size("kv")
    groups = lax.axis_size("head")
    parts = attend(queries, cache, slot_request, slot_page, lengths, w_uv)
    parts = lax.all_to_all(parts, "kv", 0, 0, tiled=True)
    values = combine(parts, requests, value_width, sections * sources)
    values = lax.all_to_all(values, ("section", "kv"), 0, 0, tiled=True)
    values = values.reshape(sections, sources, requests, value_width)
    values = values.transpose(0, 2, 1, 3).reshape(sections * requests, heads * value_width)
    projected = jnp.dot(values, w_out, preferred_element_type=jnp.float32)
    total = projected
    for step in (2, 1, 3):
        total = total + lax.ppermute(
            projected, "head", [(k, (k + step) % groups) for k in range(groups)]
        )
    return (hidden.astype(jnp.float32) + total).astype(jnp.bfloat16)


def solution(mesh):
    placed = (
        P("section", "head", None),
        P(("section", "kv"), None, None),
        P(("section", "kv")),
        P(("section", "kv")),
        P("section"),
        P("head", None, None),
        P("head", ("section", "kv")),
        P(None, ("section", "kv")),
    )
    return jax.shard_map(
        body, mesh=mesh, in_specs=placed, out_specs=P(None, ("section", "kv")), check_vma=False
    )
```

```python
import functools

import jax
import jax.numpy as jnp
from jax import lax
from jax.experimental import pallas as pl
from jax.experimental.pallas import tpu as pltpu
from jax.sharding import PartitionSpec as P

ROPE = 64
NOPE = 128
LOWEST = -1e30
UNROLL = 8
AHEAD = 4
SCAN = 16
BLIND = 16
GROUP = 16
AUX = 128
MIB = 1024 * 1024


def parts_of(value):
    high = value.astype(jnp.bfloat16).astype(jnp.float32)
    rest = value - high
    middle = rest.astype(jnp.bfloat16).astype(jnp.float32)
    return high, middle, rest - middle


def attend_kernel(
    owner_hbm, page_hbm, length_hbm, query_hbm, cache_ref, weight_hbm, out_ref,
    pages, scores, high, denom, summed, packed, values, query_ref, owner_ref, page_ref, length_ref,
    weight_ref, slots, sems, few,
):
    slot_count = cache_ref.shape[0]
    page_size = cache_ref.shape[2]
    requests, heads, _ = query_ref.shape
    latent = summed.shape[2]
    scale = (NOPE + ROPE) ** (-0.5)
    fetches = [
        pltpu.make_async_copy(source, target, few.at[k])
        for k, (source, target) in enumerate(
            (
                (owner_hbm, owner_ref),
                (page_hbm, page_ref),
                (length_hbm, length_ref),
                (query_hbm, query_ref),
                (weight_hbm, weight_ref),
            )
        )
    ]
    for fetch in fetches[:4]:
        fetch.start()

    def blind(part):
        span = pl.ds(part * UNROLL, UNROLL)
        return pltpu.make_async_copy(cache_ref.at[span], pages.at[span], sems.at[part])

    early = BLIND // UNROLL
    for part in range(early):
        blind(part).start()

    high[...] = jnp.full(high.shape, LOWEST, jnp.float32)
    denom[...] = jnp.zeros(denom.shape, jnp.float32)
    summed[...] = jnp.zeros(summed.shape, jnp.float32)
    for fetch in fetches[:3]:
        fetch.wait()

    def note(slot, found):
        alive = owner_ref[slot] >= 0
        slots[jnp.where(alive, found, slot_count - 1 - slot + found)] = slot
        return jnp.where(alive, found + 1, found)

    for k in range(UNROLL):
        slots[slot_count + k] = 0
    here = lax.fori_loop(0, BLIND, note, jnp.int32(0), unroll=SCAN)
    live = lax.fori_loop(BLIND, slot_count, note, here, unroll=SCAN)
    blocks = lax.div(live + (UNROLL - 1), jnp.int32(UNROLL))
    batches = lax.div(live - here + (UNROLL - 1), jnp.int32(UNROLL))

    def fetch_batch(batch):
        for k in range(UNROLL):
            pltpu.make_async_copy(
                cache_ref.at[slots[here + batch * UNROLL + k]],
                pages.at[BLIND + batch * UNROLL + k],
                sems.at[early + batch],
            ).start()

    def ahead(batch, carry):
        fetch_batch(batch)
        return carry

    lax.fori_loop(0, jnp.minimum(batches, AHEAD), ahead, 0)

    column = lax.broadcasted_iota(jnp.int32, (heads, page_size), 1)

    def entry_of(at):
        slot = slots[at]
        place = jnp.where(at < here, slot, BLIND - here + at)
        place = jnp.where(at < live, place, 0)
        return slot, place, lax.rem(jnp.maximum(owner_ref[slot], 0), requests)

    def arrive(batch, carry):
        @pl.when(batch + AHEAD < batches)
        def _():
            fetch_batch(batch + AHEAD)

        span = pl.ds(BLIND + batch * UNROLL, UNROLL)
        pltpu.make_async_copy(
            cache_ref.at[pl.ds(0, UNROLL)], pages.at[span], sems.at[early + batch]
        ).wait()
        return carry

    def score(block, arrived):
        first = block * UNROLL
        needed = lax.div(first + (2 * UNROLL - 1) - here, jnp.int32(UNROLL))
        needed = jnp.clip(needed, arrived, batches)
        lax.fori_loop(arrived, needed, arrive, 0)

        def keep(at, slot, mine, found):
            count = jnp.where(at < live, length_ref[mine] - page_ref[slot] * page_size, 0)
            found = jnp.where(column < count, found * scale, LOWEST)
            scores[at] = found
            high[mine] = jnp.maximum(high[mine], found)

        for k in range(UNROLL):
            slot, place, mine = entry_of(first + k)
            keep(first + k, slot, mine, jnp.dot(
                query_ref[mine], pages[place], preferred_element_type=jnp.float32
            ))
        return needed

    fetches[3].wait()
    for part in range(early):
        blind(part).wait()
    lax.fori_loop(0, blocks, score, jnp.int32(0))
    fetches[4].start()

    for mine in range(requests):
        top = jnp.max(high[mine], axis=1, keepdims=True)
        high[mine] = jnp.broadcast_to(top, (heads, page_size))

    def weigh(at):
        slot, place, mine = entry_of(at)
        weights = jnp.exp(scores[at] - high[mine])
        weights = jnp.where(at < live, weights, 0.0)
        denom[mine] += weights
        return place, mine, weights.astype(jnp.bfloat16)

    def gather(block, carry):
        first = block * UNROLL
        for k in range(0, UNROLL, 2):
            sa, ma, wa = weigh(first + k)
            sb, mb, wb = weigh(first + k + 1)
            zero = jnp.zeros_like(wa)
            lhs = jnp.concatenate([jnp.concatenate([wa, zero], axis=1), jnp.concatenate([zero, wb], axis=1)], axis=0)
            rhs = jnp.concatenate([pages[sa, :latent, :], pages[sb, :latent, :]], axis=1)
            both = lax.dot_general(lhs, rhs, (((1,), (1,)), ((), ())), preferred_element_type=jnp.float32)
            summed[ma] += both[:heads]
            summed[mb] += both[heads:]
        return carry

    lax.fori_loop(0, blocks, gather, 0)

    lane = lax.broadcasted_iota(jnp.int32, (heads, AUX), 1)
    width = weight_ref.shape[2]
    for mine in range(requests):
        packed[:, mine, :] = summed[mine]
        total = jnp.broadcast_to(jnp.sum(denom[mine], axis=1, keepdims=True), (heads, AUX))
        aux = jnp.zeros((heads, AUX), jnp.float32)
        for k, part in enumerate(parts_of(high[mine]) + parts_of(total)):
            aux = jnp.where(lane == k, part, aux)
        values[:, mine, width:] = aux
    fetches[4].wait()

    def project(block, carry):
        for k in range(GROUP):
            head = block * GROUP + k
            rows = jnp.concatenate(parts_of(packed[head]), axis=0).astype(jnp.bfloat16)
            product = jnp.dot(rows, weight_ref[head], preferred_element_type=jnp.float32)
            values[head, :, :width] = (
                product[:requests] + product[requests : 2 * requests] + product[2 * requests :]
            )
        return carry

    lax.fori_loop(0, heads // GROUP, project, 0)
    out_ref[...] = values[...].reshape(out_ref.shape).astype(jnp.bfloat16)


def attend(queries, cache, slot_request, slot_page, lengths, w_uv):
    requests, heads, width = queries.shape
    slot_count, page_size, _ = cache.shape
    padded = slot_count + UNROLL
    latent = w_uv.shape[1]
    operands = (slot_request, slot_page, lengths, queries, jnp.swapaxes(cache, 1, 2), w_uv)
    operands = [pltpu.with_memory_space_constraint(k, pltpu.HBM) for k in operands]
    vmem = pl.BlockSpec(memory_space=pltpu.VMEM)
    return pl.pallas_call(
        attend_kernel,
        out_shape=jax.ShapeDtypeStruct((heads * requests, w_uv.shape[2] + AUX), jnp.bfloat16),
        in_specs=[pl.BlockSpec(memory_space=pltpu.HBM)] * len(operands),
        out_specs=vmem,
        scratch_shapes=[
            pltpu.VMEM((slot_count, width, page_size), jnp.bfloat16),
            pltpu.VMEM((padded, heads, page_size), jnp.float32),
            pltpu.VMEM((requests, heads, page_size), jnp.float32),
            pltpu.VMEM((requests, heads, page_size), jnp.float32),
            pltpu.VMEM((requests, heads, latent), jnp.float32),
            pltpu.VMEM((heads, requests, latent), jnp.float32),
            pltpu.VMEM((heads, requests, w_uv.shape[2] + AUX), jnp.float32),
            pltpu.VMEM(queries.shape, queries.dtype),
            pltpu.SMEM(slot_request.shape, jnp.int32),
            pltpu.SMEM(slot_page.shape, jnp.int32),
            pltpu.SMEM(lengths.shape, jnp.int32),
            pltpu.VMEM(w_uv.shape, w_uv.dtype),
            pltpu.SMEM((padded,), jnp.int32),
            pltpu.SemaphoreType.DMA((padded // UNROLL,)),
            pltpu.SemaphoreType.DMA((len(operands) - 1,)),
        ],
        compiler_params=pltpu.CompilerParams(vmem_limit_bytes=28 * MIB),
        name="attend",
    )(*operands)


def combine_kernel(copies, part_ref, out_ref):
    width = out_ref.shape[1]
    requests = out_ref.shape[0] // copies
    sources = part_ref.shape[0] // requests
    aux = part_ref[:, width:].astype(jnp.float32)
    high = (aux[:, 0:1] + aux[:, 1:2] + aux[:, 2:3]).reshape(sources, requests, 1)
    denom = (aux[:, 3:4] + aux[:, 4:5] + aux[:, 5:6]).reshape(sources, requests, 1)
    factor = jnp.exp(high - jnp.max(high, axis=0, keepdims=True))
    total = jnp.sum(denom * factor, axis=0)
    parts = part_ref[:, :width].astype(jnp.float32).reshape(sources, requests, width)
    value = jnp.sum(parts * factor, axis=0) / total
    value = jnp.concatenate([value] * copies, axis=0)
    out_ref[...] = value.astype(jnp.bfloat16)


def combine(parts, requests, width, copies):
    vmem = pl.BlockSpec(memory_space=pltpu.VMEM)
    return pl.pallas_call(
        functools.partial(combine_kernel, copies),
        out_shape=jax.ShapeDtypeStruct((copies * requests, width), jnp.bfloat16),
        in_specs=[vmem],
        out_specs=vmem,
        compiler_params=pltpu.CompilerParams(vmem_limit_bytes=16 * MIB),
        name="combine",
    )(parts)


def body(queries, cache, slot_request, slot_page, lengths, w_uv, w_out, hidden):
    requests, heads, _ = queries.shape
    value_width = w_uv.shape[2]
    sections = lax.axis_size("section")
    sources = lax.axis_size("kv")
    groups = lax.axis_size("head")
    parts = attend(queries, cache, slot_request, slot_page, lengths, w_uv)
    parts = lax.all_to_all(parts, "kv", 0, 0, tiled=True)
    values = combine(parts, requests, value_width, sources)
    values = lax.all_to_all(values, "kv", 0, 0, tiled=True)
    others = lax.ppermute(values, "section", [(0, 1), (1, 0)])
    values = jnp.stack([values, others]).reshape(sections, sources, requests, value_width)
    values = values.transpose(0, 2, 1, 3).reshape(sections * requests, heads * value_width)
    projected = jnp.dot(values, w_out, preferred_element_type=jnp.float32)
    total = projected
    for step in (1, 3, 2):
        total = total + lax.ppermute(
            projected, "head", [(k, (k + step) % groups) for k in range(groups)]
        )
    swapped = jnp.concatenate([total[requests:], total[:requests]])
    total = jnp.where(lax.axis_index("section") == 0, total, swapped)
    return (hidden.astype(jnp.float32) + total).astype(jnp.bfloat16)


def solution(mesh):
    placed = (
        P("section", "head", None),
        P(("section", "kv"), None, None),
        P(("section", "kv")),
        P(("section", "kv")),
        P("section"),
        P("head", None, None),
        P("head", ("section", "kv")),
        P(None, ("section", "kv")),
    )
    return jax.shard_map(
        body, mesh=mesh, in_specs=placed, out_specs=P(None, ("section", "kv")), check_vma=False
    )
```

```python
import functools

import jax
import jax.numpy as jnp
from jax import lax
from jax.experimental import pallas as pl
from jax.experimental.pallas import tpu as pltpu
from jax.sharding import PartitionSpec as P

ROPE = 64
NOPE = 128
LOWEST = -1e30
UNROLL = 8
AHEAD = 4
WIDE = 2
SCAN = 16
BLIND = 16
GROUP = 32
AUX = 128
MIB = 1024 * 1024


def parts_of(value):
    high = value.astype(jnp.bfloat16).astype(jnp.float32)
    rest = value - high
    middle = rest.astype(jnp.bfloat16).astype(jnp.float32)
    return high, middle, rest - middle


def attend_kernel(
    owner_hbm, page_hbm, length_hbm, query_hbm, cache_ref, weight_hbm, out_ref,
    pages, scores, high, denom, summed, packed, values, query_ref, owner_ref, page_ref, length_ref,
    weight_ref, slots, sems, few,
):
    slot_count = cache_ref.shape[0]
    page_size = cache_ref.shape[2]
    requests, heads, _ = query_ref.shape
    latent = summed.shape[2]
    scale = (NOPE + ROPE) ** (-0.5)
    fetches = [
        pltpu.make_async_copy(source, target, few.at[k])
        for k, (source, target) in enumerate(
            (
                (owner_hbm, owner_ref),
                (page_hbm, page_ref),
                (length_hbm, length_ref),
                (query_hbm, query_ref),
                (weight_hbm, weight_ref),
            )
        )
    ]
    for fetch in fetches[:4]:
        fetch.start()

    def blind(part):
        span = pl.ds(part * UNROLL, UNROLL)
        return pltpu.make_async_copy(cache_ref.at[span], pages.at[span], sems.at[part])

    early = BLIND // UNROLL
    for part in range(early):
        blind(part).start()

    high[...] = jnp.full(high.shape, LOWEST, jnp.float32)
    denom[...] = jnp.zeros(denom.shape, jnp.float32)
    summed[...] = jnp.zeros(summed.shape, jnp.float32)
    for fetch in fetches[:3]:
        fetch.wait()

    def note(slot, found):
        alive = owner_ref[slot] >= 0
        slots[jnp.where(alive, found, slot_count - 1 - slot + found)] = slot
        return jnp.where(alive, found + 1, found)

    for k in range(UNROLL):
        slots[slot_count + k] = 0
    here = lax.fori_loop(0, BLIND, note, jnp.int32(0), unroll=SCAN)
    live = lax.fori_loop(BLIND, slot_count, note, here, unroll=SCAN)
    blocks = lax.div(live + (UNROLL - 1), jnp.int32(UNROLL))
    batches = lax.div(live - here + (UNROLL - 1), jnp.int32(UNROLL))

    def fetch_batch(batch):
        for k in range(UNROLL):
            pltpu.make_async_copy(
                cache_ref.at[slots[here + batch * UNROLL + k]],
                pages.at[BLIND + batch * UNROLL + k],
                sems.at[early + batch],
            ).start()

    def ahead(batch, carry):
        fetch_batch(batch)
        return carry

    lax.fori_loop(0, jnp.minimum(batches, AHEAD), ahead, 0)

    column = lax.broadcasted_iota(jnp.int32, (heads, page_size), 1)

    def entry_of(at):
        slot = slots[at]
        place = jnp.where(at < here, slot, BLIND - here + at)
        place = jnp.where(at < live, place, 0)
        return slot, place, lax.rem(jnp.maximum(owner_ref[slot], 0), requests)

    def arrive(batch, carry):
        @pl.when(batch + AHEAD < batches)
        def _():
            fetch_batch(batch + AHEAD)

        span = pl.ds(BLIND + batch * UNROLL, UNROLL)
        pltpu.make_async_copy(
            cache_ref.at[pl.ds(0, UNROLL)], pages.at[span], sems.at[early + batch]
        ).wait()
        return carry

    def score(span, first, arrived):
        needed = lax.div(first + (span + UNROLL - 1) - here, jnp.int32(UNROLL))
        needed = jnp.clip(needed, arrived, batches)
        lax.fori_loop(arrived, needed, arrive, 0)

        def keep(at, slot, mine, found):
            count = jnp.where(at < live, length_ref[mine] - page_ref[slot] * page_size, 0)
            found = jnp.where(column < count, found * scale, LOWEST)
            scores[at] = found
            high[mine] = jnp.maximum(high[mine], found)

        for k in range(span):
            slot, place, mine = entry_of(first + k)
            keep(first + k, slot, mine, jnp.dot(
                query_ref[mine], pages[place], preferred_element_type=jnp.float32
            ))
        return needed

    fetches[3].wait()
    for part in range(early):
        blind(part).wait()

    def sweep(step, carry):
        wide = lax.div(blocks, jnp.int32(WIDE))
        span = WIDE * UNROLL
        carry = lax.fori_loop(0, wide, lambda k, c: step(span, k * span, c), carry)
        return lax.fori_loop(
            wide * WIDE, blocks, lambda k, c: step(UNROLL, k * UNROLL, c), carry
        )

    sweep(score, jnp.int32(0))
    fetches[4].start()

    for mine in range(requests):
        top = jnp.max(high[mine], axis=1, keepdims=True)
        high[mine] = jnp.broadcast_to(top, (heads, page_size))

    def weigh(at):
        slot, place, mine = entry_of(at)
        weights = jnp.exp(scores[at] - high[mine])
        weights = jnp.where(at < live, weights, 0.0)
        denom[mine] += weights
        return place, mine, weights.astype(jnp.bfloat16)

    def gather(span, first, carry):
        for k in range(0, span, 2):
            sa, ma, wa = weigh(first + k)
            sb, mb, wb = weigh(first + k + 1)
            zero = jnp.zeros_like(wa)
            lhs = jnp.concatenate([jnp.concatenate([wa, zero], axis=1), jnp.concatenate([zero, wb], axis=1)], axis=0)
            rhs = jnp.concatenate([pages[sa, :latent, :], pages[sb, :latent, :]], axis=1)
            both = lax.dot_general(lhs, rhs, (((1,), (1,)), ((), ())), preferred_element_type=jnp.float32)
            summed[ma] += both[:heads]
            summed[mb] += both[heads:]
        return carry

    sweep(gather, 0)

    lane = lax.broadcasted_iota(jnp.int32, (heads, AUX), 1)
    width = weight_ref.shape[2]
    for mine in range(requests):
        packed[:, mine, :] = summed[mine]
        total = jnp.broadcast_to(jnp.sum(denom[mine], axis=1, keepdims=True), (heads, AUX))
        aux = jnp.zeros((heads, AUX), jnp.float32)
        for k, part in enumerate(parts_of(high[mine]) + parts_of(total)):
            aux = jnp.where(lane == k, part, aux)
        values[:, mine, width:] = aux
    fetches[4].wait()

    def project(block, carry):
        for k in range(GROUP):
            head = block * GROUP + k
            rows = jnp.concatenate(parts_of(packed[head]), axis=0).astype(jnp.bfloat16)
            product = jnp.dot(rows, weight_ref[head], preferred_element_type=jnp.float32)
            values[head, :, :width] = (
                product[:requests] + product[requests : 2 * requests] + product[2 * requests :]
            )
        return carry

    lax.fori_loop(0, heads // GROUP, project, 0)
    out_ref[...] = values[...].reshape(out_ref.shape).astype(jnp.bfloat16)


def attend(queries, cache, slot_request, slot_page, lengths, w_uv):
    requests, heads, width = queries.shape
    slot_count, page_size, _ = cache.shape
    padded = slot_count + UNROLL
    latent = w_uv.shape[1]
    operands = (slot_request, slot_page, lengths, queries, jnp.swapaxes(cache, 1, 2), w_uv)
    operands = [pltpu.with_memory_space_constraint(k, pltpu.HBM) for k in operands]
    vmem = pl.BlockSpec(memory_space=pltpu.VMEM)
    return pl.pallas_call(
        attend_kernel,
        out_shape=jax.ShapeDtypeStruct((heads * requests, w_uv.shape[2] + AUX), jnp.bfloat16),
        in_specs=[pl.BlockSpec(memory_space=pltpu.HBM)] * len(operands),
        out_specs=vmem,
        scratch_shapes=[
            pltpu.VMEM((slot_count, width, page_size), jnp.bfloat16),
            pltpu.VMEM((padded, heads, page_size), jnp.float32),
            pltpu.VMEM((requests, heads, page_size), jnp.float32),
            pltpu.VMEM((requests, heads, page_size), jnp.float32),
            pltpu.VMEM((requests, heads, latent), jnp.float32),
            pltpu.VMEM((heads, requests, latent), jnp.float32),
            pltpu.VMEM((heads, requests, w_uv.shape[2] + AUX), jnp.float32),
            pltpu.VMEM(queries.shape, queries.dtype),
            pltpu.SMEM(slot_request.shape, jnp.int32),
            pltpu.SMEM(slot_page.shape, jnp.int32),
            pltpu.SMEM(lengths.shape, jnp.int32),
            pltpu.VMEM(w_uv.shape, w_uv.dtype),
            pltpu.SMEM((padded,), jnp.int32),
            pltpu.SemaphoreType.DMA((padded // UNROLL,)),
            pltpu.SemaphoreType.DMA((len(operands) - 1,)),
        ],
        compiler_params=pltpu.CompilerParams(vmem_limit_bytes=28 * MIB),
        name="attend",
    )(*operands)


def combine_kernel(copies, part_ref, out_ref):
    width = out_ref.shape[1]
    requests = out_ref.shape[0] // copies
    sources = part_ref.shape[0] // requests
    aux = part_ref[:, width:].astype(jnp.float32)
    high = (aux[:, 0:1] + aux[:, 1:2] + aux[:, 2:3]).reshape(sources, requests, 1)
    denom = (aux[:, 3:4] + aux[:, 4:5] + aux[:, 5:6]).reshape(sources, requests, 1)
    factor = jnp.exp(high - jnp.max(high, axis=0, keepdims=True))
    total = jnp.sum(denom * factor, axis=0)
    parts = part_ref[:, :width].astype(jnp.float32).reshape(sources, requests, width)
    value = jnp.sum(parts * factor, axis=0) / total
    value = jnp.concatenate([value] * copies, axis=0)
    out_ref[...] = value.astype(jnp.bfloat16)


def combine(parts, requests, width, copies):
    vmem = pl.BlockSpec(memory_space=pltpu.VMEM)
    return pl.pallas_call(
        functools.partial(combine_kernel, copies),
        out_shape=jax.ShapeDtypeStruct((copies * requests, width), jnp.bfloat16),
        in_specs=[vmem],
        out_specs=vmem,
        compiler_params=pltpu.CompilerParams(vmem_limit_bytes=16 * MIB),
        name="combine",
    )(parts)


def body(queries, cache, slot_request, slot_page, lengths, w_uv, w_out, hidden):
    requests, heads, _ = queries.shape
    value_width = w_uv.shape[2]
    sections = lax.axis_size("section")
    sources = lax.axis_size("kv")
    groups = lax.axis_size("head")
    parts = attend(queries, cache, slot_request, slot_page, lengths, w_uv)
    parts = lax.all_to_all(parts, "kv", 0, 0, tiled=True)
    values = combine(parts, requests, value_width, sources)
    values = lax.all_to_all(values, "kv", 0, 0, tiled=True)
    others = lax.ppermute(values, "section", [(0, 1), (1, 0)])
    values = jnp.stack([values, others]).reshape(sections, sources, requests, value_width)
    values = values.transpose(0, 2, 1, 3).reshape(sections * requests, heads * value_width)
    projected = jnp.dot(values, w_out, preferred_element_type=jnp.float32)
    total = projected
    for step in (1, 3, 2):
        total = total + lax.ppermute(
            projected, "head", [(k, (k + step) % groups) for k in range(groups)]
        )
    swapped = jnp.concatenate([total[requests:], total[:requests]])
    total = jnp.where(lax.axis_index("section") == 0, total, swapped)
    return (hidden.astype(jnp.float32) + total).astype(jnp.bfloat16)


def solution(mesh):
    placed = (
        P("section", "head", None),
        P(("section", "kv"), None, None),
        P(("section", "kv")),
        P(("section", "kv")),
        P("section"),
        P("head", None, None),
        P("head", ("section", "kv")),
        P(None, ("section", "kv")),
    )
    return jax.shard_map(
        body, mesh=mesh, in_specs=placed, out_specs=P(None, ("section", "kv")), check_vma=False
    )
```

```python
import functools

import jax
import jax.numpy as jnp
from jax import lax
from jax.experimental import pallas as pl
from jax.experimental.pallas import tpu as pltpu
from jax.sharding import PartitionSpec as P

ROPE = 64
NOPE = 128
LOWEST = -1e30
UNROLL = 8
AHEAD = 4
WIDE = 2
SCAN = 16
BLIND = 16
GROUP = 32
AUX = 128
MIB = 1024 * 1024


def parts_of(value):
    high = value.astype(jnp.bfloat16).astype(jnp.float32)
    rest = value - high
    middle = rest.astype(jnp.bfloat16).astype(jnp.float32)
    return high, middle, rest - middle


def attend_kernel(
    owner_hbm, page_hbm, length_hbm, query_hbm, cache_ref, weight_hbm, out_ref,
    pages, scores, high, denom, summed, packed, values, query_ref, owner_ref, page_ref, length_ref,
    weight_ref, slots, sems, few,
):
    slot_count = cache_ref.shape[0]
    page_size = cache_ref.shape[2]
    requests, heads, _ = query_ref.shape
    latent = summed.shape[2]
    scale = (NOPE + ROPE) ** (-0.5)
    fetches = [
        pltpu.make_async_copy(source, target, few.at[k])
        for k, (source, target) in enumerate(
            (
                (owner_hbm, owner_ref),
                (page_hbm, page_ref),
                (length_hbm, length_ref),
                (query_hbm, query_ref),
                (weight_hbm, weight_ref),
            )
        )
    ]
    for fetch in fetches[:4]:
        fetch.start()

    def blind(part):
        span = pl.ds(part * UNROLL, UNROLL)
        return pltpu.make_async_copy(cache_ref.at[span], pages.at[span], sems.at[part])

    early = BLIND // UNROLL
    for part in range(early):
        blind(part).start()

    high[...] = jnp.full(high.shape, LOWEST, jnp.float32)
    denom[...] = jnp.zeros(denom.shape, jnp.float32)
    summed[...] = jnp.zeros(summed.shape, jnp.float32)
    for fetch in fetches[:3]:
        fetch.wait()

    def note(slot, found):
        alive = owner_ref[slot] >= 0
        slots[jnp.where(alive, found, slot_count - 1 - slot + found)] = slot
        return jnp.where(alive, found + 1, found)

    for k in range(UNROLL):
        slots[slot_count + k] = 0
    here = lax.fori_loop(0, BLIND, note, jnp.int32(0), unroll=SCAN)
    live = lax.fori_loop(BLIND, slot_count, note, here, unroll=SCAN)
    blocks = lax.div(live + (UNROLL - 1), jnp.int32(UNROLL))
    batches = lax.div(live - here + (UNROLL - 1), jnp.int32(UNROLL))

    def fetch_batch(batch):
        for k in range(UNROLL):
            pltpu.make_async_copy(
                cache_ref.at[slots[here + batch * UNROLL + k]],
                pages.at[BLIND + batch * UNROLL + k],
                sems.at[early + batch],
            ).start()

    def ahead(batch, carry):
        fetch_batch(batch)
        return carry

    lax.fori_loop(0, jnp.minimum(batches, AHEAD), ahead, 0)

    column = lax.broadcasted_iota(jnp.int32, (heads, page_size), 1)

    def entry_of(at):
        slot = slots[at]
        place = jnp.where(at < here, slot, BLIND - here + at)
        place = jnp.where(at < live, place, 0)
        return slot, place, lax.rem(jnp.maximum(owner_ref[slot], 0), requests)

    def arrive(batch, carry):
        @pl.when(batch + AHEAD < batches)
        def _():
            fetch_batch(batch + AHEAD)

        span = pl.ds(BLIND + batch * UNROLL, UNROLL)
        pltpu.make_async_copy(
            cache_ref.at[pl.ds(0, UNROLL)], pages.at[span], sems.at[early + batch]
        ).wait()
        return carry

    def score(span, first, arrived):
        needed = lax.div(first + (span + UNROLL - 1) - here, jnp.int32(UNROLL))
        needed = jnp.clip(needed, arrived, batches)
        lax.fori_loop(arrived, needed, arrive, 0)

        def keep(at, slot, mine, found):
            count = jnp.where(at < live, length_ref[mine] - page_ref[slot] * page_size, 0)
            found = jnp.where(column < count, found * scale, LOWEST)
            scores[at] = found
            high[mine] = jnp.maximum(high[mine], found)

        for k in range(span):
            slot, place, mine = entry_of(first + k)
            keep(first + k, slot, mine, jnp.dot(
                query_ref[mine], pages[place], preferred_element_type=jnp.float32
            ))
        return needed

    fetches[3].wait()
    for part in range(early):
        blind(part).wait()

    def sweep(step, carry, between=None):
        wide = lax.div(blocks, jnp.int32(WIDE))
        span = WIDE * UNROLL
        carry = lax.fori_loop(0, wide, lambda k, c: step(span, k * span, c), carry)
        if between is not None:
            between()
        return lax.fori_loop(
            wide * WIDE, blocks, lambda k, c: step(UNROLL, k * UNROLL, c), carry
        )

    sweep(score, jnp.int32(0), fetches[4].start)

    for mine in range(requests):
        top = jnp.max(high[mine], axis=1, keepdims=True)
        high[mine] = jnp.broadcast_to(top, (heads, page_size))

    def weigh(at):
        slot, place, mine = entry_of(at)
        weights = jnp.exp(scores[at] - high[mine])
        weights = jnp.where(at < live, weights, 0.0)
        denom[mine] += weights
        return place, mine, weights.astype(jnp.bfloat16)

    def gather(span, first, carry):
        for k in range(0, span, 2):
            sa, ma, wa = weigh(first + k)
            sb, mb, wb = weigh(first + k + 1)
            zero = jnp.zeros_like(wa)
            lhs = jnp.concatenate([jnp.concatenate([wa, zero], axis=1), jnp.concatenate([zero, wb], axis=1)], axis=0)
            rhs = jnp.concatenate([pages[sa, :latent, :], pages[sb, :latent, :]], axis=1)
            both = lax.dot_general(lhs, rhs, (((1,), (1,)), ((), ())), preferred_element_type=jnp.float32)
            summed[ma] += both[:heads]
            summed[mb] += both[heads:]
        return carry

    sweep(gather, 0)

    lane = lax.broadcasted_iota(jnp.int32, (heads, AUX), 1)
    width = weight_ref.shape[2]
    for mine in range(requests):
        packed[:, mine, :] = summed[mine]
        total = jnp.broadcast_to(jnp.sum(denom[mine], axis=1, keepdims=True), (heads, AUX))
        aux = jnp.zeros((heads, AUX), jnp.float32)
        for k, part in enumerate(parts_of(high[mine]) + parts_of(total)):
            aux = jnp.where(lane == k, part, aux)
        values[:, mine, width:] = aux
    fetches[4].wait()

    def project(block, carry):
        for k in range(GROUP):
            head = block * GROUP + k
            rows = jnp.concatenate(parts_of(packed[head]), axis=0).astype(jnp.bfloat16)
            product = jnp.dot(rows, weight_ref[head], preferred_element_type=jnp.float32)
            values[head, :, :width] = (
                product[:requests] + product[requests : 2 * requests] + product[2 * requests :]
            )
        return carry

    lax.fori_loop(0, heads // GROUP, project, 0)
    out_ref[...] = values[...].reshape(out_ref.shape).astype(jnp.bfloat16)


def attend(queries, cache, slot_request, slot_page, lengths, w_uv):
    requests, heads, width = queries.shape
    slot_count, page_size, _ = cache.shape
    padded = slot_count + UNROLL
    latent = w_uv.shape[1]
    operands = (slot_request, slot_page, lengths, queries, jnp.swapaxes(cache, 1, 2), w_uv)
    operands = [pltpu.with_memory_space_constraint(k, pltpu.HBM) for k in operands]
    vmem = pl.BlockSpec(memory_space=pltpu.VMEM)
    return pl.pallas_call(
        attend_kernel,
        out_shape=jax.ShapeDtypeStruct((heads * requests, w_uv.shape[2] + AUX), jnp.bfloat16),
        in_specs=[pl.BlockSpec(memory_space=pltpu.HBM)] * len(operands),
        out_specs=vmem,
        scratch_shapes=[
            pltpu.VMEM((slot_count, width, page_size), jnp.bfloat16),
            pltpu.VMEM((padded, heads, page_size), jnp.float32),
            pltpu.VMEM((requests, heads, page_size), jnp.float32),
            pltpu.VMEM((requests, heads, page_size), jnp.float32),
            pltpu.VMEM((requests, heads, latent), jnp.float32),
            pltpu.VMEM((heads, requests, latent), jnp.float32),
            pltpu.VMEM((heads, requests, w_uv.shape[2] + AUX), jnp.float32),
            pltpu.VMEM(queries.shape, queries.dtype),
            pltpu.SMEM(slot_request.shape, jnp.int32),
            pltpu.SMEM(slot_page.shape, jnp.int32),
            pltpu.SMEM(lengths.shape, jnp.int32),
            pltpu.VMEM(w_uv.shape, w_uv.dtype),
            pltpu.SMEM((padded,), jnp.int32),
            pltpu.SemaphoreType.DMA((padded // UNROLL,)),
            pltpu.SemaphoreType.DMA((len(operands) - 1,)),
        ],
        compiler_params=pltpu.CompilerParams(vmem_limit_bytes=28 * MIB),
        name="attend",
    )(*operands)


def combine_kernel(copies, part_ref, out_ref):
    width = out_ref.shape[1]
    requests = out_ref.shape[0] // copies
    sources = part_ref.shape[0] // requests
    aux = part_ref[:, width:].astype(jnp.float32)
    high = (aux[:, 0:1] + aux[:, 1:2] + aux[:, 2:3]).reshape(sources, requests, 1)
    denom = (aux[:, 3:4] + aux[:, 4:5] + aux[:, 5:6]).reshape(sources, requests, 1)
    factor = jnp.exp(high - jnp.max(high, axis=0, keepdims=True))
    total = jnp.sum(denom * factor, axis=0)
    parts = part_ref[:, :width].astype(jnp.float32).reshape(sources, requests, width)
    value = jnp.sum(parts * factor, axis=0) / total
    value = jnp.concatenate([value] * copies, axis=0)
    out_ref[...] = value.astype(jnp.bfloat16)


def combine(parts, requests, width, copies):
    vmem = pl.BlockSpec(memory_space=pltpu.VMEM)
    return pl.pallas_call(
        functools.partial(combine_kernel, copies),
        out_shape=jax.ShapeDtypeStruct((copies * requests, width), jnp.bfloat16),
        in_specs=[vmem],
        out_specs=vmem,
        compiler_params=pltpu.CompilerParams(vmem_limit_bytes=16 * MIB),
        name="combine",
    )(parts)


def body(queries, cache, slot_request, slot_page, lengths, w_uv, w_out, hidden):
    requests, heads, _ = queries.shape
    value_width = w_uv.shape[2]
    sections = lax.axis_size("section")
    sources = lax.axis_size("kv")
    groups = lax.axis_size("head")
    parts = attend(queries, cache, slot_request, slot_page, lengths, w_uv)
    parts = lax.all_to_all(parts, "kv", 0, 0, tiled=True)
    values = combine(parts, requests, value_width, sources)
    values = lax.all_to_all(values, "kv", 0, 0, tiled=True)
    others = lax.ppermute(values, "section", [(0, 1), (1, 0)])
    values = jnp.stack([values, others]).reshape(sections, sources, requests, value_width)
    values = values.transpose(0, 2, 1, 3).reshape(sections * requests, heads * value_width)
    projected = jnp.dot(values, w_out, preferred_element_type=jnp.float32)
    total = projected
    for step in (1, 3, 2):
        total = total + lax.ppermute(
            projected, "head", [(k, (k + step) % groups) for k in range(groups)]
        )
    swapped = jnp.concatenate([total[requests:], total[:requests]])
    total = jnp.where(lax.axis_index("section") == 0, total, swapped)
    return (hidden.astype(jnp.float32) + total).astype(jnp.bfloat16)


def solution(mesh):
    placed = (
        P("section", "head", None),
        P(("section", "kv"), None, None),
        P(("section", "kv")),
        P(("section", "kv")),
        P("section"),
        P("head", None, None),
        P("head", ("section", "kv")),
        P(None, ("section", "kv")),
    )
    return jax.shard_map(
        body, mesh=mesh, in_specs=placed, out_specs=P(None, ("section", "kv")), check_vma=False
    )
```

```python
import functools

import jax
import jax.numpy as jnp
from jax import lax
from jax.experimental import pallas as pl
from jax.experimental.pallas import tpu as pltpu
from jax.sharding import PartitionSpec as P

ROPE = 64
NOPE = 128
LOWEST = -1e30
UNROLL = 8
AHEAD = 4
WIDE = 2
SCAN = 16
BLIND = 16
GROUP = 32
AUX = 128
MIB = 1024 * 1024


def parts_of(value):
    high = value.astype(jnp.bfloat16).astype(jnp.float32)
    rest = value - high
    middle = rest.astype(jnp.bfloat16).astype(jnp.float32)
    return high, middle, rest - middle


def attend_kernel(
    owner_hbm, page_hbm, length_hbm, query_hbm, cache_ref, weight_hbm, out_ref,
    pages, scores, high, denom, summed, packed, values, query_ref, owner_ref, page_ref, length_ref,
    weight_ref, slots, sems, few,
):
    slot_count = cache_ref.shape[0]
    page_size = cache_ref.shape[2]
    requests, heads, _ = query_ref.shape
    latent = summed.shape[2]
    scale = (NOPE + ROPE) ** (-0.5)
    fetches = [
        pltpu.make_async_copy(source, target, few.at[k])
        for k, (source, target) in enumerate(
            (
                (owner_hbm, owner_ref),
                (page_hbm, page_ref),
                (length_hbm, length_ref),
                (query_hbm, query_ref),
                (weight_hbm, weight_ref),
            )
        )
    ]
    for fetch in fetches[:4]:
        fetch.start()

    def blind(part):
        span = pl.ds(part * UNROLL, UNROLL)
        return pltpu.make_async_copy(cache_ref.at[span], pages.at[span], sems.at[part])

    early = BLIND // UNROLL
    for part in range(early):
        blind(part).start()

    high[...] = jnp.full(high.shape, LOWEST, jnp.float32)
    denom[...] = jnp.zeros(denom.shape, jnp.float32)
    summed[...] = jnp.zeros(summed.shape, jnp.float32)
    for fetch in fetches[:3]:
        fetch.wait()

    def note(slot, found):
        alive = owner_ref[slot] >= 0
        slots[jnp.where(alive, found, slot_count - 1 - slot + found)] = slot
        return jnp.where(alive, found + 1, found)

    for k in range(UNROLL):
        slots[slot_count + k] = 0
    here = lax.fori_loop(0, BLIND, note, jnp.int32(0), unroll=SCAN)
    live = lax.fori_loop(BLIND, slot_count, note, here, unroll=SCAN)
    blocks = lax.div(live + (UNROLL - 1), jnp.int32(UNROLL))
    batches = lax.div(live - here + (UNROLL - 1), jnp.int32(UNROLL))

    def fetch_batch(batch):
        for k in range(UNROLL):
            pltpu.make_async_copy(
                cache_ref.at[slots[here + batch * UNROLL + k]],
                pages.at[BLIND + batch * UNROLL + k],
                sems.at[early + batch],
            ).start()

    def ahead(batch, carry):
        fetch_batch(batch)
        return carry

    lax.fori_loop(0, jnp.minimum(batches, AHEAD), ahead, 0)

    column = lax.broadcasted_iota(jnp.int32, (heads, page_size), 1)

    def entry_of(at):
        slot = slots[at]
        place = jnp.where(at < here, slot, BLIND - here + at)
        place = jnp.where(at < live, place, 0)
        return slot, place, lax.rem(jnp.maximum(owner_ref[slot], 0), requests)

    def arrive(batch, carry):
        @pl.when(batch + AHEAD < batches)
        def _():
            fetch_batch(batch + AHEAD)

        span = pl.ds(BLIND + batch * UNROLL, UNROLL)
        pltpu.make_async_copy(
            cache_ref.at[pl.ds(0, UNROLL)], pages.at[span], sems.at[early + batch]
        ).wait()
        return carry

    def score(span, first, arrived):
        needed = lax.div(first + (span + UNROLL - 1) - here, jnp.int32(UNROLL))
        needed = jnp.clip(needed, arrived, batches)
        lax.fori_loop(arrived, needed, arrive, 0)

        def keep(at, slot, mine, found):
            count = jnp.where(at < live, length_ref[mine] - page_ref[slot] * page_size, 0)
            found = jnp.where(column < count, found * scale, LOWEST)
            scores[at] = found
            high[mine] = jnp.maximum(high[mine], found)

        for k in range(span):
            slot, place, mine = entry_of(first + k)
            keep(first + k, slot, mine, jnp.dot(
                query_ref[mine], pages[place], preferred_element_type=jnp.float32
            ))
        return needed

    fetches[3].wait()
    for part in range(early):
        blind(part).wait()

    def sweep(step, carry, between=None):
        wide = lax.div(blocks, jnp.int32(WIDE))
        span = WIDE * UNROLL
        carry = lax.fori_loop(0, wide, lambda k, c: step(span, k * span, c), carry)
        if between is not None:
            between()
        return lax.fori_loop(
            wide * WIDE, blocks, lambda k, c: step(UNROLL, k * UNROLL, c), carry
        )

    sweep(score, jnp.int32(0), fetches[4].start)

    for mine in range(requests):
        top = jnp.max(high[mine], axis=1, keepdims=True)
        high[mine] = jnp.broadcast_to(top, (heads, page_size))

    def weigh(at):
        slot, place, mine = entry_of(at)
        weights = jnp.exp(scores[at] - high[mine])
        weights = jnp.where(at < live, weights, 0.0)
        denom[mine] += weights
        return place, mine, weights.astype(jnp.bfloat16)

    def gather(span, first, carry):
        for k in range(0, span, 2):
            sa, ma, wa = weigh(first + k)
            sb, mb, wb = weigh(first + k + 1)
            zero = jnp.zeros_like(wa)
            lhs = jnp.concatenate([jnp.concatenate([wa, zero], axis=1), jnp.concatenate([zero, wb], axis=1)], axis=0)
            rhs = jnp.concatenate([pages[sa, :latent, :], pages[sb, :latent, :]], axis=1)
            both = lax.dot_general(lhs, rhs, (((1,), (1,)), ((), ())), preferred_element_type=jnp.float32)
            summed[ma] += both[:heads]
            summed[mb] += both[heads:]
        return carry

    sweep(gather, 0)

    lane = lax.broadcasted_iota(jnp.int32, (heads, AUX), 1)
    width = weight_ref.shape[2]
    for mine in range(requests):
        packed[:, mine, :] = summed[mine]
        total = jnp.broadcast_to(jnp.sum(denom[mine], axis=1, keepdims=True), (heads, AUX))
        aux = jnp.zeros((heads, AUX), jnp.float32)
        for k, part in enumerate(parts_of(high[mine]) + parts_of(total)):
            aux = jnp.where(lane == k, part, aux)
        values[:, mine, width:] = aux
    fetches[4].wait()

    def project(block, carry):
        for k in range(GROUP):
            head = block * GROUP + k
            value = packed[head]
            top = value.astype(jnp.bfloat16).astype(jnp.float32)
            rows = jnp.concatenate([top, value - top], axis=0).astype(jnp.bfloat16)
            product = jnp.dot(rows, weight_ref[head], preferred_element_type=jnp.float32)
            values[head, :, :width] = product[:requests] + product[requests:]
        return carry

    lax.fori_loop(0, heads // GROUP, project, 0)
    out_ref[...] = values[...].reshape(out_ref.shape).astype(jnp.bfloat16)


def attend(queries, cache, slot_request, slot_page, lengths, w_uv):
    requests, heads, width = queries.shape
    slot_count, page_size, _ = cache.shape
    padded = slot_count + UNROLL
    latent = w_uv.shape[1]
    operands = (slot_request, slot_page, lengths, queries, jnp.swapaxes(cache, 1, 2), w_uv)
    operands = [pltpu.with_memory_space_constraint(k, pltpu.HBM) for k in operands]
    vmem = pl.BlockSpec(memory_space=pltpu.VMEM)
    return pl.pallas_call(
        attend_kernel,
        out_shape=jax.ShapeDtypeStruct((heads * requests, w_uv.shape[2] + AUX), jnp.bfloat16),
        in_specs=[pl.BlockSpec(memory_space=pltpu.HBM)] * len(operands),
        out_specs=vmem,
        scratch_shapes=[
            pltpu.VMEM((slot_count, width, page_size), jnp.bfloat16),
            pltpu.VMEM((padded, heads, page_size), jnp.float32),
            pltpu.VMEM((requests, heads, page_size), jnp.float32),
            pltpu.VMEM((requests, heads, page_size), jnp.float32),
            pltpu.VMEM((requests, heads, latent), jnp.float32),
            pltpu.VMEM((heads, requests, latent), jnp.float32),
            pltpu.VMEM((heads, requests, w_uv.shape[2] + AUX), jnp.float32),
            pltpu.VMEM(queries.shape, queries.dtype),
            pltpu.SMEM(slot_request.shape, jnp.int32),
            pltpu.SMEM(slot_page.shape, jnp.int32),
            pltpu.SMEM(lengths.shape, jnp.int32),
            pltpu.VMEM(w_uv.shape, w_uv.dtype),
            pltpu.SMEM((padded,), jnp.int32),
            pltpu.SemaphoreType.DMA((padded // UNROLL,)),
            pltpu.SemaphoreType.DMA((len(operands) - 1,)),
        ],
        compiler_params=pltpu.CompilerParams(vmem_limit_bytes=28 * MIB),
        name="attend",
    )(*operands)


def combine_kernel(copies, part_ref, out_ref):
    width = out_ref.shape[1]
    requests = out_ref.shape[0] // copies
    sources = part_ref.shape[0] // requests
    aux = part_ref[:, width:].astype(jnp.float32)
    high = (aux[:, 0:1] + aux[:, 1:2] + aux[:, 2:3]).reshape(sources, requests, 1)
    denom = (aux[:, 3:4] + aux[:, 4:5] + aux[:, 5:6]).reshape(sources, requests, 1)
    factor = jnp.exp(high - jnp.max(high, axis=0, keepdims=True))
    total = jnp.sum(denom * factor, axis=0)
    parts = part_ref[:, :width].astype(jnp.float32).reshape(sources, requests, width)
    value = jnp.sum(parts * factor, axis=0) / total
    value = jnp.concatenate([value] * copies, axis=0)
    out_ref[...] = value.astype(jnp.bfloat16)


def combine(parts, requests, width, copies):
    vmem = pl.BlockSpec(memory_space=pltpu.VMEM)
    return pl.pallas_call(
        functools.partial(combine_kernel, copies),
        out_shape=jax.ShapeDtypeStruct((copies * requests, width), jnp.bfloat16),
        in_specs=[vmem],
        out_specs=vmem,
        compiler_params=pltpu.CompilerParams(vmem_limit_bytes=16 * MIB),
        name="combine",
    )(parts)


def body(queries, cache, slot_request, slot_page, lengths, w_uv, w_out, hidden):
    requests, heads, _ = queries.shape
    value_width = w_uv.shape[2]
    sections = lax.axis_size("section")
    sources = lax.axis_size("kv")
    groups = lax.axis_size("head")
    parts = attend(queries, cache, slot_request, slot_page, lengths, w_uv)
    parts = lax.all_to_all(parts, "kv", 0, 0, tiled=True)
    values = combine(parts, requests, value_width, sources)
    values = lax.all_to_all(values, "kv", 0, 0, tiled=True)
    others = lax.ppermute(values, "section", [(0, 1), (1, 0)])
    values = jnp.stack([values, others]).reshape(sections, sources, requests, value_width)
    values = values.transpose(0, 2, 1, 3).reshape(sections * requests, heads * value_width)
    projected = jnp.dot(values, w_out, preferred_element_type=jnp.float32)
    total = projected
    for step in (1, 3, 2):
        total = total + lax.ppermute(
            projected, "head", [(k, (k + step) % groups) for k in range(groups)]
        )
    swapped = jnp.concatenate([total[requests:], total[:requests]])
    total = jnp.where(lax.axis_index("section") == 0, total, swapped)
    return (hidden.astype(jnp.float32) + total).astype(jnp.bfloat16)


def solution(mesh):
    placed = (
        P("section", "head", None),
        P(("section", "kv"), None, None),
        P(("section", "kv")),
        P(("section", "kv")),
        P("section"),
        P("head", None, None),
        P("head", ("section", "kv")),
        P(None, ("section", "kv")),
    )
    return jax.shard_map(
        body, mesh=mesh, in_specs=placed, out_specs=P(None, ("section", "kv")), check_vma=False
    )
```
